128 devices in a mesh: dp: 32 (over y, z, core), vocab: 4 (over x).
Axes of the slice: x: 4, y: 4, z: 4, core: 2. Of those that a mesh axis runs over, the one named last changes fastest.
Arguments:
- token_grads: bfloat16 [32768, 5376], P(('dp', 'vocab')), may hold values from -24 to 24
- row_holder: int32 [32768, 1], P(('dp', 'vocab')), may hold values from 0 to 127; in each aligned block of 256 rows (0 to 255, 256 to 511, ...) at most 3 rows name the same one
- row_offset: int32 [32768], P(('dp', 'vocab')), may hold values from 0 to 255
- table: bfloat16 [32768, 5376], P(('dp', 'vocab')), may hold values from -6 to 6
- first_moment: bfloat16 [32768, 5376], P(('dp', 'vocab')), may hold values from -3 to 3
- second_moment: bfloat16 [32768, 5376], P(('dp', 'vocab')), may hold values from 0.049804688 to 4
Outputs:
- new_table: bfloat16 [32768, 5376], P(('dp', 'vocab'))
- new_first: bfloat16 [32768, 5376], P(('dp', 'vocab'))
- new_second: bfloat16 [32768, 5376], P(('dp', 'vocab'))
The draws below stay inside these ranges and needn't reach their ends.
Inputs may be any that keep to these rules, and one draw needn't show every extreme that they name: `row_holder`: among the tokens of one device, at most 3 name the same holder, and some device has a holder named exactly 3 times.
All inputs are finite; a program needn't handle non-finite values.
Results may differ from the reference program's by a relative error of at most 0.0004.
Values may be sent and summed in bfloat16 or wider, within the bound.
No kernel may reach another device: no remote copies, remote signals or barrier semaphores. Data moves between devices by JAX's collectives and lax.ppermute only.
A program may use at most 128 MiB of HBM per device.

```python
import math
import jax
import jax.numpy as jnp
import numpy as np

D = 5376
TOK_DEV = 256
ROWS_DEV = 256
CAP = 3
TOKENS = 32768
VOCAB = 32768
DEVICES = 128


def draw_token_grads(key, part):
    key = jax.random.fold_in(key, 7)
    noise_key, common_key = jax.random.split(key, 2)
    noise = jax.random.normal(noise_key, (TOKENS, D), jnp.float32)
    common = jax.random.normal(common_key, (1, D), jnp.float32)
    values = 2.0 * (noise + common)
    return jnp.clip(values, -24.0, 24.0).astype(jnp.bfloat16)


def place_ends(array, rng, least, top_value):
    spot = [jax.random.randint(jax.random.fold_in(rng, axis), (), 0, length) for axis, length in enumerate(array.shape)]
    longest = array.shape.index(max(array.shape))
    next_to = spot[:longest] + [(spot[longest] + 1) % array.shape[longest]] + spot[longest + 1:]
    return array.at[tuple(spot)].set(least).at[tuple(next_to)].set(top_value)


def block_levels(stream_key, shape, pieces, smallest, top_value):
    gain = 1.0
    for position, parts in pieces:
        steps = jax.random.uniform(jax.random.fold_in(jax.random.fold_in(stream_key, 6), position), (parts,), jnp.float32, smallest / len(pieces), top_value / len(pieces))
        gain = gain * jnp.repeat(jnp.exp(steps), shape[position] // parts).reshape((-1,) + (1,) * (len(shape) - 1 - position))
    return gain


def assign_block(stream_key, own, number, rows, amount, top, most, skew):
    order = jax.random.permutation(stream_key, amount)
    packed, usual = shares(amount, rows * top, most, skew, True), shares(amount, rows * top, most, skew, False)
    places = jnp.arange(amount)

    def named(lengths, rotation):
        used = int((lengths > 0).sum())
        fixed = max(1, used // 4)
        moved = fixed + (places - fixed + rotation * (used - fixed)) % max(1, amount - fixed)
        return jnp.zeros((amount,), jnp.int32).at[order[jnp.where(places < fixed, places, moved)]].set(jnp.asarray(lengths, jnp.int32))

    lengths = jnp.where(number % 4 == 0, named(packed, number // 4), named(usual, number - number // 4 - 1))
    mixed = jax.random.permutation(jax.random.fold_in(own, 3), amount)
    donor, taker = mixed[0:amount // 2 * 2:2], mixed[1:amount // 2 * 2:2]
    room = jnp.minimum(lengths[donor] - 1, most - lengths[taker]) // 2
    room = jnp.where((donor == order[0]) | (taker == order[0]) | (lengths[taker] == 0), 0, jnp.maximum(room, 0))
    moved = jax.random.randint(jax.random.fold_in(own, 4), (amount // 2,), 0, 1 << 20) % (room + 1)
    lengths = lengths.at[donor].add(-moved).at[taker].add(moved)
    members = jnp.searchsorted(jnp.cumsum(lengths), jnp.arange(rows * top), side="right").astype(jnp.int32)
    grid = members.reshape(top, rows).T
    grid = grid[jax.random.permutation(jax.random.fold_in(own, 1), rows)]
    rotation = jax.random.randint(jax.random.fold_in(own, 2), (rows, 1), 0, top)
    return jnp.take_along_axis(grid, (jnp.arange(top)[None, :] + rotation) % top, axis=1)


def shares(count, total, most, skew, full):
    portions = [(1 << 20) // math.isqrt(grade ** skew) + 1 for grade in range(1, count + 1)]
    largest = most if full else min(most, max(-(-total // count), total * portions[0] // sum(portions)))
    least = 1 if total - largest >= count - 1 else 0
    given, surplus = [largest] + [least] * (count - 1), total - largest - least * (count - 1)
    while surplus > 0:
        movable = [i for i in range(1, count) if given[i] < largest] or [i for i in range(1, count) if given[i] < most]
        pool, left = sum([portions[i] for i in movable]), surplus
        for i in movable:
            extra = min(most - given[i], max(1, left * portions[i] // pool), surplus)
            given[i] = given[i] + extra
            surplus = surplus - extra
    return np.array(given)


def centred(stream_key, shape, scale, reach, cuts=(), dtype=jnp.bfloat16):
    result = jax.random.normal(stream_key, shape, jnp.float32) * scale
    if len(cuts) > 0:
        result = block_levels(stream_key, shape, cuts, -0.22, 0.18) * result
    return jnp.clip(result, min=-reach, max=reach).astype(dtype)


def setup_inputs(seed: int = 0) -> dict:
    key_of = jax.random.split(jax.random.key(seed), 7)
    token_grads = draw_token_grads(jax.random.fold_in(key_of[6], 71), 0)
    row_holder_keys = jax.random.split(jax.random.fold_in(key_of[1], 1), TOKENS // TOK_DEV)
    row_holder_turns = jax.random.permutation(jax.random.fold_in(key_of[1], 3), TOKENS // TOK_DEV)
    row_holder = jax.vmap(lambda own, number: assign_block(jax.random.fold_in(key_of[1], 2), own, number, TOK_DEV, DEVICES, 1, CAP, 1))(row_holder_keys, row_holder_turns).reshape((TOKENS, 1))
    row_offset = place_ends(jax.random.randint(key_of[2], (TOKENS,), 0, ROWS_DEV), jax.random.fold_in(key_of[2], 1), 0, ROWS_DEV - 1).astype(jnp.int32)
    table = centred(key_of[3], (VOCAB, D), 1.0, 6.0, ((0, 128),))
    first_moment = centred(key_of[4], (VOCAB, D), 0.5, 3.0, ((0, 128),))
    second_moment = jnp.clip(jnp.exp(math.log(4.0) - 4.3859405 * jax.random.uniform(key_of[5], (VOCAB, D), jnp.float32) ** block_levels(key_of[5], (VOCAB, D), ((0, 128),), -0.2, 0.2)), 0.049804688, 4.0).astype(jnp.bfloat16)
    return {"token_grads": token_grads, "row_holder": row_holder, "row_offset": row_offset, "table": table, "first_moment": first_moment, "second_moment": second_moment}


def reference(token_grads, row_holder, row_offset, table, first_moment, second_moment):
    row_id = (row_holder[:, 0] * ROWS_DEV + row_offset).astype(jnp.int32)
    grad_sum = jax.ops.segment_sum(token_grads.astype(jnp.float32), row_id, num_segments=VOCAB)
    total = jnp.sum(grad_sum * grad_sum)
    limit = 2.0 * jnp.sqrt(jnp.float32(TOKENS * D))
    factor = jnp.minimum(jnp.float32(1.0), limit / jnp.sqrt(total))
    grad = factor * grad_sum
    first = 0.9 * first_moment.astype(jnp.float32) + 0.1 * grad
    second = 0.95 * second_moment.astype(jnp.float32) + 0.05 * grad * grad
    step_size = first / (1.0 - 0.9 ** 10) / (jnp.sqrt(second / (1.0 - 0.95 ** 10)) + 1e-08)
    new_table = (table.astype(jnp.float32) - 0.02 * step_size).astype(jnp.bfloat16)
    return (new_table, first.astype(jnp.bfloat16), second.astype(jnp.bfloat16))
```

```python
import jax
import jax.numpy as jnp
from jax import lax
from jax.experimental import pallas as pl
from jax.experimental.pallas import tpu as pltpu
from jax.sharding import PartitionSpec as P

AXES = ("dp", "vocab")
SLOTS = 3
CELL = 256
ROWS = 8
BF = jnp.bfloat16
F32 = jnp.float32


def cell_of(piece, slot):
    if piece < 16:
        return piece // 2, 3 * (piece % 2) + slot
    entry = 3 * (piece - 16) + slot
    return entry // 2, 6 + entry % 2


def pattern(piece, column):
    return tuple((cell_of(piece, s)[1], s) for s in range(SLOTS) if cell_of(piece, s)[0] == column)


def iota(shape, dim):
    return lax.broadcasted_iota(jnp.int32, shape, dim)


def pack_kernel(n_dev, holder_ref, offset_ref, grads_ref, out_ref):
    toks = grads_ref.shape[0]
    pieces = grads_ref.shape[1] // CELL
    columns = out_ref.shape[1] // CELL
    holder = holder_ref[...]
    holder_f = holder.astype(F32)
    holder_col = jnp.broadcast_to(holder_f, (128, toks)).T
    halves = []
    for h in range(toks // 128):
        same = (holder_col == holder_f[:, h * 128:(h + 1) * 128]) & (
            iota((toks, 128), 0) < iota((toks, 128), 1) + h * 128)
        halves.append(jnp.sum(same.astype(F32), axis=0, keepdims=True))
    rank_f = jnp.concatenate(halves, axis=1)
    rank = rank_f.astype(jnp.int32)
    rank_col = jnp.broadcast_to(rank_f, (128, toks)).T
    lane = iota((toks, 128), 1).astype(F32)
    rank_hot = jnp.where(rank_col == lane, 1.0, 0.0).astype(BF)
    rank_hot = jnp.concatenate([rank_hot, jnp.zeros_like(rank_hot)], axis=1)
    offset_value = (offset_ref[...] + 1).astype(F32)
    row = iota((n_dev * ROWS, toks), 0)

    def one_hot(pat):
        place = jnp.full((1, toks), -1, jnp.int32)
        for r, s in pat:
            place = jnp.where(rank == s, holder * ROWS + r, place)
        return jnp.where(row == place, 1.0, 0.0).astype(BF)

    made = {}

    def get(pat):
        if pat not in made:
            made[pat] = one_hot(pat)
        return made[pat]

    for k in range(columns):
        left, right = [], []
        for p in range(pieces):
            pat = pattern(p, k)
            if pat:
                left.append(get(pat))
                right.append(grads_ref[:, p * CELL:(p + 1) * CELL])
        if k == columns - 1:
            left.append(jnp.where(row == holder * ROWS + ROWS - 1, offset_value, 0.0).astype(BF))
            right.append(rank_hot)
        out_ref[:, k * CELL:(k + 1) * CELL] = jnp.dot(
            jnp.concatenate(left, axis=1), jnp.concatenate(right, axis=0),
            preferred_element_type=F32).astype(BF)


def sum_kernel(n_dev, arrived_ref, grad_ref, part_ref, wide_ref):
    rows_here = grad_ref.shape[0]
    pieces = grad_ref.shape[1] // CELL
    columns = arrived_ref.shape[1] // CELL
    depth = n_dev * ROWS
    wide_ref[...] = arrived_ref[:, (columns - 1) * CELL:(columns - 1) * CELL + 128].astype(F32)
    tail = wide_ref[pl.ds(ROWS - 1, n_dev, stride=ROWS), :]
    spread = jnp.where(iota((n_dev, depth), 0) == iota((n_dev, depth), 1) // ROWS, 1.0, 0.0).astype(BF)
    target = jnp.dot(tail.T.astype(BF), spread, preferred_element_type=F32).astype(jnp.int32) - 1
    place = iota((1, depth), 1) % ROWS
    row = iota((rows_here, depth), 0)
    made = {}

    def get(pat):
        if pat not in made:
            wanted = jnp.full((1, depth), -1, jnp.int32)
            for r, s in pat:
                wanted = jnp.where(place == r, target[s:s + 1, :], wanted)
            made[pat] = jnp.where(row == wanted, 1.0, 0.0).astype(BF)
        return made[pat]

    total = jnp.zeros((8, CELL), F32)
    for p in range(pieces):
        left, right = [], []
        for k in range(columns):
            pat = pattern(p, k)
            if pat:
                left.append(get(pat))
                right.append(arrived_ref[:, k * CELL:(k + 1) * CELL])
        piece = jnp.dot(jnp.concatenate(left, axis=1), jnp.concatenate(right, axis=0),
                        preferred_element_type=F32)
        grad_ref[:, p * CELL:(p + 1) * CELL] = piece
        total = total + jnp.sum((piece * piece).reshape(rows_here // 8, 8, CELL), axis=0)
    folded = total[:, :128] + total[:, 128:]
    part_ref[...] = jnp.broadcast_to(jnp.sum(folded, axis=0, keepdims=True), part_ref.shape)


def adam_kernel(limit, sums_ref, grad_ref, table_ref, first_ref, second_ref, ot_ref, of_ref, os_ref):
    total = jnp.sum(jnp.sum(sums_ref[...], axis=0, keepdims=True), axis=1, keepdims=True)
    factor = jnp.minimum(1.0, limit / jnp.sqrt(total))
    grad = factor * grad_ref[...]
    first = 0.9 * first_ref[...].astype(F32) + 0.1 * grad
    second = 0.95 * second_ref[...].astype(F32) + 0.05 * grad * grad
    step = first * (0.02 / (1.0 - 0.9**10)) / (jnp.sqrt(second * (1.0 / (1.0 - 0.95**10))) + 1e-8)
    ot_ref[...] = (table_ref[...].astype(F32) - step).astype(BF)
    of_ref[...] = first.astype(BF)
    os_ref[...] = second.astype(BF)


def body(token_grads, row_holder, row_offset, table, first_moment, second_moment):
    n_dev = lax.axis_size("dp") * lax.axis_size("vocab")
    toks, width = token_grads.shape
    rows_here = table.shape[0]
    depth = n_dev * ROWS
    lanes = 8 * CELL
    vmem = pl.BlockSpec(memory_space=pltpu.VMEM)

    with jax.named_scope("pack"):
        outgoing = pl.pallas_call(
            lambda *refs: pack_kernel(n_dev, *refs),
            out_shape=jax.ShapeDtypeStruct((depth, lanes), BF),
            in_specs=[vmem] * 3, out_specs=vmem,
            compiler_params=pltpu.CompilerParams(vmem_limit_bytes=40 * 2**20),
        )(row_holder.reshape(1, toks), row_offset.reshape(1, toks), token_grads)
    with jax.named_scope("exchange"):
        arrived = lax.all_to_all(outgoing, AXES, split_axis=0, concat_axis=0, tiled=True)
    with jax.named_scope("row_sums"):
        grad_sum, part = pl.pallas_call(
            lambda *refs: sum_kernel(n_dev, *refs),
            out_shape=(jax.ShapeDtypeStruct((rows_here, width), F32),
                       jax.ShapeDtypeStruct((n_dev, 128), F32)),
            in_specs=[vmem], out_specs=(vmem, vmem),
            scratch_shapes=[pltpu.VMEM((depth, 128), F32)],
            compiler_params=pltpu.CompilerParams(vmem_limit_bytes=40 * 2**20),
        )(arrived)
    with jax.named_scope("norm"):
        sums = lax.all_to_all(part, AXES, split_axis=0, concat_axis=0, tiled=True)
    limit = 2.0 * float(toks * n_dev * width) ** 0.5
    tall = 32
    block = pl.BlockSpec((tall, width), lambda i: (i, 0))
    with jax.named_scope("adam"):
        return pl.pallas_call(
            lambda *refs: adam_kernel(limit, *refs),
            grid=(rows_here // tall,),
            out_shape=(jax.ShapeDtypeStruct((rows_here, width), BF),) * 3,
            in_specs=[pl.BlockSpec((n_dev, 128), lambda i: (0, 0))] + [block] * 4,
            out_specs=(block,) * 3,
            compiler_params=pltpu.CompilerParams(vmem_limit_bytes=40 * 2**20),
        )(sums, grad_sum, table, first_moment, second_moment)


def solution(mesh):
    rows = P(AXES, None)
    return jax.shard_map(
        body, mesh=mesh,
        in_specs=(rows, rows, P(AXES), rows, rows, rows),
        out_specs=(rows, rows, rows), check_vma=False)
```

```python
import jax
import jax.numpy as jnp
from jax import lax
from jax.experimental import pallas as pl
from jax.experimental.pallas import tpu as pltpu
from jax.sharding import PartitionSpec as P

AXES = ("dp", "vocab")
SLOTS = 3
CELL = 256
ROWS = 8
TALL = 16
WIDE = 384
BF = jnp.bfloat16
F32 = jnp.float32


def cell_of(piece, slot):
    if piece < 16:
        return piece // 2, 3 * (piece % 2) + slot
    entry = 3 * (piece - 16) + slot
    return entry // 2, 6 + entry % 2


def pattern(piece, column):
    return tuple((cell_of(piece, s)[1], s) for s in range(SLOTS) if cell_of(piece, s)[0] == column)


def iota(shape, dim):
    return lax.broadcasted_iota(jnp.int32, shape, dim)


def pack_kernel(n_dev, holder_hbm, offset_hbm, grads_hbm, out_ref, holder_ref, offset_ref, grads_ref, sems, wide_ref):
    moves = [pltpu.make_async_copy(a, b, sems.at[i]) for i, (a, b) in enumerate(
        ((holder_hbm, holder_ref), (offset_hbm, offset_ref), (grads_hbm, grads_ref)))]
    for move in moves:
        move.start()
    moves[0].wait()
    moves[1].wait()
    toks = grads_ref.shape[0]
    pieces = grads_ref.shape[1] // CELL
    columns = out_ref.shape[1] // CELL
    depth = out_ref.shape[0]
    holder = holder_ref[...]
    holder_f = holder.astype(F32)
    holder_col = jnp.broadcast_to(holder_f, (128, toks)).T
    halves = []
    for h in range(toks // 128):
        same = (holder_col == holder_f[:, h * 128:(h + 1) * 128]) & (
            iota((toks, 128), 0) < iota((toks, 128), 1) + h * 128)
        halves.append(jnp.sum(same.astype(F32), axis=0, keepdims=True))
    rank_f = jnp.concatenate(halves, axis=1)
    rank = rank_f.astype(jnp.int32)
    rank_col = jnp.broadcast_to(rank_f, (128, toks)).T
    lane = iota((toks, 128), 1).astype(F32)
    rank_hot = jnp.where(rank_col == lane, 1.0, 0.0).astype(BF)
    rank_hot = jnp.concatenate([rank_hot, jnp.zeros_like(rank_hot)], axis=1)
    offset_value = (offset_ref[...] + 1).astype(F32)
    row = iota((n_dev, toks), 0)
    hot = jnp.concatenate([
        jnp.where(row == jnp.where(rank == s, holder, -1), 1.0, 0.0).astype(BF) for s in range(SLOTS)], axis=0)
    offset_hot = jnp.where(row == holder, offset_value, 0.0).astype(BF)
    moves[2].wait()

    def put(piece, slot, value):
        column, r = cell_of(piece, slot)
        for c in range(0, CELL, 128):
            wide_ref[pl.ds((column * CELL + c) // 128 * depth + r, n_dev, stride=ROWS), :] = value[:, c:c + 128]

    order = sorted(range(pieces), key=lambda p: (max(cell_of(p, s)[0] for s in range(SLOTS)), p))
    done = 0
    put(pieces, 0, jnp.dot(offset_hot, rank_hot, preferred_element_type=F32))
    for i, p in enumerate(order):
        got = jnp.dot(hot, grads_ref[:, p * CELL:(p + 1) * CELL], preferred_element_type=F32)
        for s in range(SLOTS):
            put(p, s, got[s * n_dev:(s + 1) * n_dev])
        ready = min([cell_of(q, s)[0] for q in order[i + 1:] for s in range(SLOTS)] + [columns])
        if ready > done:
            for t in range(done * CELL // 128, ready * CELL // 128):
                out_ref[:, t * 128:(t + 1) * 128] = wide_ref[t * depth:(t + 1) * depth, :].astype(BF)
            done = ready


def sum_kernel(n_dev, arrived_ref, grad_ref, part_ref, wide_ref):
    rows_here = grad_ref.shape[0]
    pieces = grad_ref.shape[1] // CELL
    columns = arrived_ref.shape[1] // CELL
    depth = arrived_ref.shape[0]

    def take(piece, slot):
        column, r = cell_of(piece, slot)
        return jnp.concatenate([
            wide_ref[pl.ds((column * CELL + c) // 128 * depth + r, n_dev, stride=ROWS), :]
            for c in range(0, CELL, 128)], axis=1)


    def widen(column):
        for t in range(column * CELL // 128, (column + 1) * CELL // 128):
            wide_ref[t * depth:(t + 1) * depth, :] = arrived_ref[:, t * 128:(t + 1) * 128].astype(F32)

    widen(columns - 1)
    target = take(pieces, 0)[:, :128].T.astype(jnp.int32) - 1
    row = iota((rows_here, n_dev), 0)
    hot = jnp.concatenate([
        jnp.where(row == target[s:s + 1, :], 1.0, 0.0).astype(BF) for s in range(SLOTS)], axis=1)
    total = jnp.zeros((8, CELL), F32)
    widened = 0
    order = sorted(range(pieces), key=lambda p: (max(cell_of(p, s)[0] for s in range(SLOTS)), p))
    for p in order:
        need = max(cell_of(p, s)[0] for s in range(SLOTS)) + 1
        for k in range(widened, min(need, columns - 1)):
            widen(k)
        widened = max(widened, need)
        right = jnp.concatenate([take(p, s).astype(BF) for s in range(SLOTS)], axis=0)
        piece = jnp.dot(hot, right, preferred_element_type=F32)
        grad_ref[:, p * CELL:(p + 1) * CELL] = piece
        total = total + jnp.sum((piece * piece).reshape(rows_here // 8, 8, CELL), axis=0)
    folded = total[:, :128] + total[:, 128:]
    part_ref[...] = jnp.broadcast_to(jnp.sum(folded, axis=0, keepdims=True), part_ref.shape)


def adam_kernel(limit, sums_ref, grad_ref, table_ref, first_ref, second_ref, ot_ref, of_ref, os_ref,
                st_ref, sf_ref, ss_ref, sems):
    rows_here, width = grad_ref.shape
    total = jnp.sum(jnp.sum(sums_ref[...], axis=0, keepdims=True), axis=1, keepdims=True)
    factor = jnp.minimum(1.0, limit / jnp.sqrt(total))
    first_gain = 0.1 * factor
    second_gain = 0.05 * (factor * factor)
    root = (1.0 / (1.0 - 0.95**10)) ** 0.5
    scale = 0.02 / (1.0 - 0.9**10) / root
    tiny = 1e-8 / root

    def send(i, what, start):
        return pltpu.make_async_copy(
            (st_ref, sf_ref, ss_ref)[what].at[pl.ds(start, TALL)],
            (ot_ref, of_ref, os_ref)[what].at[pl.ds(start, TALL)], sems.at[what, i])

    def step(i, _):
        start = pl.multiple_of(i * TALL, TALL)
        rows = pl.ds(start, TALL)
        for c in range(0, width, WIDE):
            cols = slice(c, c + WIDE)
            grad = grad_ref[rows, cols]
            first = 0.9 * first_ref[rows, cols].astype(F32) + first_gain * grad
            second = 0.95 * second_ref[rows, cols].astype(F32) + second_gain * (grad * grad)
            bottom = second * lax.rsqrt(second) + tiny
            moved = (scale * first) * pl.reciprocal(bottom, approx=True)
            st_ref[rows, cols] = (table_ref[rows, cols].astype(F32) - moved).astype(BF)
            sf_ref[rows, cols] = first.astype(BF)
            ss_ref[rows, cols] = second.astype(BF)
        for what in range(3):
            send(i, what, start).start()
        return 0

    steps = rows_here // TALL
    lax.fori_loop(0, steps, step, 0)
    for i in range(steps):
        for what in range(3):
            send(i, what, i * TALL).wait()


def body(token_grads, row_holder, row_offset, table, first_moment, second_moment):
    n_dev = lax.axis_size("dp") * lax.axis_size("vocab")
    toks, width = token_grads.shape
    rows_here = table.shape[0]
    depth = n_dev * ROWS
    lanes = 8 * CELL
    vmem = pl.BlockSpec(memory_space=pltpu.VMEM)

    with jax.named_scope("pack"):
        outgoing = pl.pallas_call(
            lambda *refs: pack_kernel(n_dev, *refs),
            out_shape=jax.ShapeDtypeStruct((depth, lanes), BF),
            in_specs=[pl.BlockSpec(memory_space=pltpu.HBM)] * 3, out_specs=vmem,
            scratch_shapes=[pltpu.VMEM((1, toks), jnp.int32), pltpu.VMEM((1, toks), jnp.int32),
                            pltpu.VMEM((toks, width), BF), pltpu.SemaphoreType.DMA((3,)), pltpu.VMEM((lanes // 128 * depth, 128), F32)],
            compiler_params=pltpu.CompilerParams(vmem_limit_bytes=40 * 2**20),
        )(*(pltpu.with_memory_space_constraint(a, pltpu.HBM) for a in (row_holder.reshape(1, toks), row_offset.reshape(1, toks), token_grads)))
    with jax.named_scope("exchange"):
        arrived = lax.all_to_all(outgoing, AXES, split_axis=0, concat_axis=0, tiled=True)
    with jax.named_scope("row_sums"):
        grad_sum, part = pl.pallas_call(
            lambda *refs: sum_kernel(n_dev, *refs),
            out_shape=(jax.ShapeDtypeStruct((rows_here, width), F32),
                       jax.ShapeDtypeStruct((n_dev, 128), F32)),
            in_specs=[vmem], out_specs=(vmem, vmem),
            scratch_shapes=[pltpu.VMEM((lanes // 128 * depth, 128), F32)],
            compiler_params=pltpu.CompilerParams(vmem_limit_bytes=40 * 2**20),
        )(arrived)
    with jax.named_scope("norm"):
        sums = lax.all_to_all(part, AXES, split_axis=0, concat_axis=0, tiled=True)
    limit = 2.0 * float(toks * n_dev * width) ** 0.5
    out = pl.BlockSpec(memory_space=pltpu.HBM)
    with jax.named_scope("adam"):
        return pl.pallas_call(
            lambda *refs: adam_kernel(limit, *refs),
            out_shape=(jax.ShapeDtypeStruct((rows_here, width), BF),) * 3,
            in_specs=[vmem] * 5, out_specs=(out,) * 3,
            scratch_shapes=[pltpu.VMEM((rows_here, width), BF)] * 3
            + [pltpu.SemaphoreType.DMA((3, rows_here // TALL))],
            compiler_params=pltpu.CompilerParams(vmem_limit_bytes=30 * 2**20),
        )(sums, grad_sum, table, first_moment, second_moment)


def solution(mesh):
    rows = P(AXES, None)
    return jax.shard_map(
        body, mesh=mesh,
        in_specs=(rows, rows, P(AXES), rows, rows, rows),
        out_specs=(rows, rows, rows), check_vma=False)
```

```python
import jax
import jax.numpy as jnp
import numpy as np
from jax import lax
from jax.experimental import pallas as pl
from jax.experimental.pallas import tpu as pltpu
from jax.sharding import PartitionSpec as P

AXES = ("dp", "vocab")
SLOTS = 3
CELL = 256
ROWS = 8
LOADS = (0, 9)
PITCH = 133
TALL = 16
WIDE = 256
BF = jnp.bfloat16
F32 = jnp.float32

OFFSETS = -1


def cell_of(piece, slot):
    if piece < 5:
        entry = 15 if piece == OFFSETS else 3 * piece + slot
        return entry // 2, 6 + entry % 2
    return (piece - 5) // 2, 3 * ((piece - 5) % 2) + slot


def iota(shape, dim):
    return lax.broadcasted_iota(jnp.int32, shape, dim)


def pack_kernel(n_dev, holder_hbm, offset_hbm, grads_hbm, out_ref, holder_ref, offset_ref, grads_ref, sems, *wide_refs):
    toks = grads_ref.shape[0]
    pieces = grads_ref.shape[1] // CELL
    moves = [pltpu.make_async_copy(a, b, sems.at[pieces + i]) for i, (a, b) in enumerate(
        ((holder_hbm, holder_ref), (offset_hbm, offset_ref)))]
    loads = {}
    ends = list(LOADS) + [pieces]
    for p, end in zip(ends, ends[1:]):
        cols = slice(p * CELL, end * CELL)
        loads[p] = pltpu.make_async_copy(grads_hbm.at[:, cols], grads_ref.at[:, cols], sems.at[p])
    for move in moves + list(loads.values())[:1]:
        move.start()
    for move in moves:
        move.wait()
    for load in list(loads.values())[1:]:
        load.start()
    columns = out_ref.shape[1] // CELL
    depth = out_ref.shape[0]
    holder = holder_ref[...]
    holder_f = holder.astype(F32)
    holder_col = jnp.broadcast_to(holder_f, (128, toks)).T
    halves = []
    for h in range(toks // 128):
        same = (holder_col == holder_f[:, h * 128:(h + 1) * 128]) & (
            iota((toks, 128), 0) < iota((toks, 128), 1) + h * 128)
        halves.append(jnp.sum(same.astype(F32), axis=0, keepdims=True))
    rank_f = jnp.concatenate(halves, axis=1)
    rank = rank_f.astype(jnp.int32)
    rank_col = jnp.broadcast_to(rank_f, (128, toks)).T
    lane = iota((toks, 128), 1).astype(F32)
    rank_hot = jnp.where(rank_col == lane, 1.0, 0.0).astype(BF)
    rank_hot = jnp.concatenate([rank_hot, jnp.zeros_like(rank_hot)], axis=1)
    offset_value = (offset_ref[...] + 1).astype(F32)
    row = iota((n_dev, toks), 0)
    hot = jnp.concatenate([
        jnp.where(row == jnp.where(rank == s, holder, -1), 1.0, 0.0).astype(BF) for s in range(SLOTS)], axis=0)
    offset_hot = jnp.where(row == holder, offset_value, 0.0).astype(BF)

    def put(piece, slot, value):
        column, r = cell_of(piece, slot)
        for c in range(0, CELL, 128):
            wide_refs[column][pl.ds(c // 128 * depth + r, n_dev, stride=ROWS), :] = value[:, c:c + 128]

    done = 0
    put(OFFSETS, 0, jnp.dot(offset_hot, rank_hot, preferred_element_type=F32))
    for p in range(pieces):
        if p in loads:
            loads[p].wait()
        got = jnp.dot(hot, grads_ref[:, p * CELL:(p + 1) * CELL], preferred_element_type=F32)
        for s in range(SLOTS):
            put(p, s, got[s * n_dev:(s + 1) * n_dev])
        ready = min([cell_of(q, s)[0] for q in range(p + 1, pieces) for s in range(SLOTS)] + [columns])
        for column in range(done, ready):
            for row0 in range(0, depth, 64):
                out_ref[row0:row0 + 64, column * CELL:(column + 1) * CELL] = jnp.concatenate(
                    [wide_refs[column][t * depth + row0:t * depth + row0 + 64, :] for t in range(CELL // 128)],
                    axis=1).astype(BF)
        done = max(done, ready)


def sum_kernel(n_dev, arrived_ref, grad_ref, part_ref, *wide_refs):
    rows_here = grad_ref.shape[0]
    pieces = grad_ref.shape[1] // CELL
    columns = arrived_ref.shape[1] // CELL
    depth = arrived_ref.shape[0]

    def take(piece, slot):
        column, r = cell_of(piece, slot)
        return jnp.concatenate([
            wide_refs[column][(c // 128 * ROWS + r) * PITCH:(c // 128 * ROWS + r) * PITCH + n_dev, :]
            for c in range(0, CELL, 128)], axis=1)

    def widen(column):
        both = arrived_ref[:, column * CELL:(column + 1) * CELL].astype(F32)
        for t in range(CELL // 128):
            for source in range(n_dev):
                wide_refs[column][pl.ds(t * ROWS * PITCH + source, ROWS, stride=PITCH), :] = both[
                    source * ROWS:(source + 1) * ROWS, t * 128:(t + 1) * 128]

    widen(columns - 1)
    target = take(OFFSETS, 0)[:, :128].T.astype(jnp.int32) - 1
    row = iota((rows_here, n_dev), 0)
    hot = jnp.concatenate([
        jnp.where(row == target[s:s + 1, :], 1.0, 0.0).astype(BF) for s in range(SLOTS)], axis=1)
    total = jnp.zeros((8, CELL), F32)
    widened = 0
    for p in list(range(5, pieces)) + list(range(5)):
        need = max(cell_of(p, s)[0] for s in range(SLOTS)) + 1
        for k in range(widened, min(need, columns - 1)):
            widen(k)
        widened = max(widened, need)
        right = jnp.concatenate([take(p, s).astype(BF) for s in range(SLOTS)], axis=0)
        piece = jnp.dot(hot, right, preferred_element_type=F32)
        grad_ref[:, p * CELL:(p + 1) * CELL] = piece
        total = total + jnp.sum((piece * piece).reshape(rows_here // 8, 8, CELL), axis=0)
    folded = total[:, :128] + total[:, 128:]
    part_ref[...] = jnp.broadcast_to(jnp.sum(folded, axis=0, keepdims=True), part_ref.shape)


def adam_kernel(limit, sums_ref, grad_ref, first_ref, second_ref, table_ref, ot_ref, of_ref, os_ref,
                st_ref, sf_ref, ss_ref, sems):
    rows_here, width = grad_ref.shape
    total = jnp.sum(jnp.sum(sums_ref[...], axis=0, keepdims=True), axis=1, keepdims=True)
    factor = jnp.minimum(1.0, limit / jnp.sqrt(total))
    first_gain = 0.1 * factor
    second_gain = 0.05 * (factor * factor)
    root = (1.0 / (1.0 - 0.95**10)) ** 0.5
    scale = 0.02 / (1.0 - 0.9**10) / root
    tiny = 1e-8 / root

    def scaled(matrix, values):
        return jnp.dot(matrix, jnp.concatenate([values] * 3, axis=0), preferred_element_type=F32)

    def times(value):
        parts, value = [], float(np.float32(value))
        for _ in range(3):
            parts.insert(0, float(np.float32(value).astype(BF)))
            value -= parts[0]
        row, column = iota((TALL, 3 * TALL), 0), iota((TALL, 3 * TALL), 1)
        which = jnp.where(column < TALL, parts[0], jnp.where(column < 2 * TALL, parts[1], parts[2]))
        return jnp.where(row == column % TALL, which, 0.0).astype(BF)

    first_mat, second_mat = times(0.9), times(0.95)

    def send(i, what):
        rows = pl.ds(i * TALL, TALL)
        return pltpu.make_async_copy(
            (st_ref, sf_ref, ss_ref)[what].at[rows], (ot_ref, of_ref, os_ref)[what].at[rows], sems.at[what, i])

    for i in range(rows_here // TALL):
        rows = slice(i * TALL, (i + 1) * TALL)
        for c in range(0, width, WIDE):
            cols = slice(c, c + WIDE)
            grad = grad_ref[rows, cols]
            first = scaled(first_mat, first_ref[rows, cols]) + first_gain * grad
            second = scaled(second_mat, second_ref[rows, cols]) + second_gain * (grad * grad)
            bottom = second * lax.rsqrt(second) + tiny
            moved = (scale * first) * pl.reciprocal(bottom, approx=True)
            st_ref[rows, cols] = (table_ref[rows, cols].astype(F32) - moved).astype(BF)
            sf_ref[rows, cols] = first.astype(BF)
            ss_ref[rows, cols] = second.astype(BF)
        for what in range(3):
            send(i, what).start()
    for i in range(rows_here // TALL):
        for what in range(3):
            send(i, what).wait()


def body(token_grads, row_holder, row_offset, table, first_moment, second_moment):
    n_dev = lax.axis_size("dp") * lax.axis_size("vocab")
    toks, width = token_grads.shape
    rows_here = table.shape[0]
    depth = n_dev * ROWS
    lanes = 8 * CELL
    vmem = pl.BlockSpec(memory_space=pltpu.VMEM)

    with jax.named_scope("pack"):
        outgoing = pl.pallas_call(
            lambda *refs: pack_kernel(n_dev, *refs),
            out_shape=jax.ShapeDtypeStruct((depth, lanes), BF),
            in_specs=[pl.BlockSpec(memory_space=pltpu.HBM)] * 3, out_specs=vmem,
            scratch_shapes=[pltpu.VMEM((1, toks), jnp.int32), pltpu.VMEM((1, toks), jnp.int32),
                            pltpu.VMEM((toks, width), BF), pltpu.SemaphoreType.DMA((width // CELL + 2,))]
            + [pltpu.VMEM((CELL // 128 * depth, 128), F32)] * (lanes // CELL),
            compiler_params=pltpu.CompilerParams(vmem_limit_bytes=40 * 2**20),
        )(*(pltpu.with_memory_space_constraint(a, pltpu.HBM) for a in (
            row_holder.reshape(1, toks), row_offset.reshape(1, toks), token_grads)))
    with jax.named_scope("exchange"):
        arrived = lax.all_to_all(outgoing, AXES, split_axis=0, concat_axis=0, tiled=True)
    with jax.named_scope("row_sums"):
        grad_sum, part = pl.pallas_call(
            lambda *refs: sum_kernel(n_dev, *refs),
            out_shape=(jax.ShapeDtypeStruct((rows_here, width), F32),
                       jax.ShapeDtypeStruct((n_dev, 128), F32)),
            in_specs=[vmem], out_specs=(vmem, vmem),
            scratch_shapes=[pltpu.VMEM((CELL // 128 * ROWS * PITCH, 128), F32)] * (lanes // CELL),
            compiler_params=pltpu.CompilerParams(vmem_limit_bytes=40 * 2**20),
        )(arrived)
    with jax.named_scope("norm"):
        sums = lax.all_to_all(part, AXES, split_axis=0, concat_axis=0, tiled=True)
    limit = 2.0 * float(toks * n_dev * width) ** 0.5
    out = pl.BlockSpec(memory_space=pltpu.HBM)
    with jax.named_scope("adam"):
        return pl.pallas_call(
            lambda *refs: adam_kernel(limit, *refs),
            out_shape=(jax.ShapeDtypeStruct((rows_here, width), BF),) * 3,
            in_specs=[vmem] * 5, out_specs=(out,) * 3,
            scratch_shapes=[pltpu.VMEM((rows_here, width), BF)] * 3
            + [pltpu.SemaphoreType.DMA((3, rows_here // TALL))],
            compiler_params=pltpu.CompilerParams(vmem_limit_bytes=30 * 2**20),
        )(sums, grad_sum, first_moment, second_moment, table)


def solution(mesh):
    rows = P(AXES, None)
    return jax.shard_map(
        body, mesh=mesh,
        in_specs=(rows, rows, P(AXES), rows, rows, rows),
        out_specs=(rows, rows, rows), check_vma=False)
```

```python
import jax
import jax.numpy as jnp
import numpy as np
from jax import lax
from jax.experimental import pallas as pl
from jax.experimental.pallas import tpu as pltpu
from jax.sharding import PartitionSpec as P

AXES = ("dp", "vocab")
SLOTS = 3
CELL = 256
ROWS = 8
LOADS = (0, 9)
PITCH = 133
TALL = 16
WIDE = 256
BF = jnp.bfloat16
F32 = jnp.float32

OFFSETS = -1


def cell_of(piece, slot):
    if piece < 5:
        entry = 15 if piece == OFFSETS else 3 * piece + slot
        return entry // 2, 6 + entry % 2
    return (piece - 5) // 2, 3 * ((piece - 5) % 2) + slot


def iota(shape, dim):
    return lax.broadcasted_iota(jnp.int32, shape, dim)


def pack_kernel(n_dev, holder_hbm, offset_hbm, grads_hbm, out_ref, holder_ref, offset_ref, grads_ref, sems, *wide_refs):
    toks = grads_ref.shape[0]
    pieces = grads_ref.shape[1] // CELL
    moves = [pltpu.make_async_copy(a, b, sems.at[pieces + i]) for i, (a, b) in enumerate(
        ((holder_hbm, holder_ref), (offset_hbm, offset_ref)))]
    loads = {}
    ends = list(LOADS) + [pieces]
    for p, end in zip(ends, ends[1:]):
        cols = slice(p * CELL, end * CELL)
        loads[p] = pltpu.make_async_copy(grads_hbm.at[:, cols], grads_ref.at[:, cols], sems.at[p])
    for move in moves + list(loads.values())[:1]:
        move.start()
    for move in moves:
        move.wait()
    for load in list(loads.values())[1:]:
        load.start()
    columns = out_ref.shape[1] // CELL
    depth = out_ref.shape[0]
    holder = holder_ref[...]
    holder_f = holder.astype(F32)
    holder_col = jnp.broadcast_to(holder_f, (128, toks)).T
    halves = []
    for h in range(toks // 128):
        same = (holder_col == holder_f[:, h * 128:(h + 1) * 128]) & (
            iota((toks, 128), 0) < iota((toks, 128), 1) + h * 128)
        halves.append(jnp.sum(same.astype(F32), axis=0, keepdims=True))
    rank_f = jnp.concatenate(halves, axis=1)
    rank = rank_f.astype(jnp.int32)
    rank_col = jnp.broadcast_to(rank_f, (128, toks)).T
    lane = iota((toks, 128), 1).astype(F32)
    rank_hot = jnp.where(rank_col == lane, 1.0, 0.0).astype(BF)
    rank_hot = jnp.concatenate([rank_hot, jnp.zeros_like(rank_hot)], axis=1)
    offset_value = (offset_ref[...] + 1).astype(F32)
    row = iota((n_dev, toks), 0)
    hot = jnp.concatenate([
        jnp.where(row == jnp.where(rank == s, holder, -1), 1.0, 0.0).astype(BF) for s in range(SLOTS)], axis=0)
    offset_hot = jnp.where(row == holder, offset_value, 0.0).astype(BF)

    def put(piece, slot, value):
        column, r = cell_of(piece, slot)
        for c in range(0, CELL, 128):
            wide_refs[column][pl.ds(c // 128 * depth + r, n_dev, stride=ROWS), :] = value[:, c:c + 128]

    done = 0
    put(OFFSETS, 0, jnp.dot(offset_hot, rank_hot, preferred_element_type=F32))
    for p in range(pieces):
        if p in loads:
            loads[p].wait()
        got = jnp.dot(hot, grads_ref[:, p * CELL:(p + 1) * CELL], preferred_element_type=F32)
        for s in range(SLOTS):
            put(p, s, got[s * n_dev:(s + 1) * n_dev])
        ready = min([cell_of(q, s)[0] for q in range(p + 1, pieces) for s in range(SLOTS)] + [columns])
        for column in range(done, ready):
            for row0 in range(0, depth, 64):
                out_ref[row0:row0 + 64, column * CELL:(column + 1) * CELL] = jnp.concatenate(
                    [wide_refs[column][t * depth + row0:t * depth + row0 + 64, :] for t in range(CELL // 128)],
                    axis=1).astype(BF)
        done = max(done, ready)


def sum_kernel(n_dev, arrived_ref, grad_ref, part_ref, *wide_refs):
    rows_here = grad_ref.shape[0]
    pieces = grad_ref.shape[1] // CELL
    columns = arrived_ref.shape[1] // CELL
    depth = arrived_ref.shape[0]

    def take(piece, slot):
        column, r = cell_of(piece, slot)
        return jnp.concatenate([
            wide_refs[column][(c // 128 * ROWS + r) * PITCH:(c // 128 * ROWS + r) * PITCH + n_dev, :]
            for c in range(0, CELL, 128)], axis=1)

    def widen(column):
        both = arrived_ref[:, column * CELL:(column + 1) * CELL].astype(F32)
        for t in range(CELL // 128):
            for source in range(n_dev):
                wide_refs[column][pl.ds(t * ROWS * PITCH + source, ROWS, stride=PITCH), :] = both[
                    source * ROWS:(source + 1) * ROWS, t * 128:(t + 1) * 128]

    widen(columns - 1)
    target = take(OFFSETS, 0)[:, :128].T.astype(jnp.int32) - 1
    row = iota((rows_here, n_dev), 0)
    hot = jnp.concatenate([
        jnp.where(row == target[s:s + 1, :], 1.0, 0.0).astype(BF) for s in range(SLOTS)], axis=1)
    total = jnp.zeros((8, CELL), F32)
    widened = 0
    for p in list(range(5, pieces)) + list(range(5)):
        need = max(cell_of(p, s)[0] for s in range(SLOTS)) + 1
        for k in range(widened, min(need, columns - 1)):
            widen(k)
        widened = max(widened, need)
        right = jnp.concatenate([take(p, s).astype(BF) for s in range(SLOTS)], axis=0)
        piece = jnp.dot(hot, right, preferred_element_type=F32)
        grad_ref[:, p * CELL:(p + 1) * CELL] = piece
        total = total + jnp.sum((piece * piece).reshape(rows_here // 8, 8, CELL), axis=0)
    folded = total[:, :128] + total[:, 128:]
    part_ref[...] = jnp.broadcast_to(jnp.sum(jnp.sum(folded, axis=0, keepdims=True), axis=1, keepdims=True), part_ref.shape)


def adam_kernel(limit, sums_ref, grad_ref, first_ref, second_ref, table_ref, ot_ref, of_ref, os_ref,
                st_ref, sf_ref, ss_ref, sems):
    rows_here, width = grad_ref.shape
    total = jnp.sum(sums_ref[...], axis=0, keepdims=True)[:, :1]
    factor = jnp.minimum(1.0, limit * lax.rsqrt(total))
    first_gain = 0.1 * factor
    second_gain = 0.05 * (factor * factor)
    root = (1.0 / (1.0 - 0.95**10)) ** 0.5
    scale = 0.02 / (1.0 - 0.9**10) / root
    tiny = 1e-8 / root

    def scaled(matrix, values):
        return jnp.dot(matrix, jnp.concatenate([values] * 3, axis=0), preferred_element_type=F32)

    def times(value):
        parts, value = [], float(np.float32(value))
        for _ in range(3):
            parts.insert(0, float(np.float32(value).astype(BF)))
            value -= parts[0]
        row, column = iota((TALL, 3 * TALL), 0), iota((TALL, 3 * TALL), 1)
        which = jnp.where(column < TALL, parts[0], jnp.where(column < 2 * TALL, parts[1], parts[2]))
        return jnp.where(row == column % TALL, which, 0.0).astype(BF)

    first_mat, second_mat = times(0.9), times(0.95)

    def send(i, what):
        rows = pl.ds(i * TALL, TALL)
        return pltpu.make_async_copy(
            (st_ref, sf_ref, ss_ref)[what].at[rows], (ot_ref, of_ref, os_ref)[what].at[rows], sems.at[what, i])

    for i in range(rows_here // TALL):
        rows = slice(i * TALL, (i + 1) * TALL)
        for c in range(0, width, WIDE):
            cols = slice(c, c + WIDE)
            grad = grad_ref[rows, cols]
            first = scaled(first_mat, first_ref[rows, cols]) + first_gain * grad
            second = scaled(second_mat, second_ref[rows, cols]) + second_gain * (grad * grad)
            bottom = second * lax.rsqrt(second) + tiny
            moved = (scale * first) * pl.reciprocal(bottom, approx=True)
            st_ref[rows, cols] = (table_ref[rows, cols].astype(F32) - moved).astype(BF)
            sf_ref[rows, cols] = first.astype(BF)
            ss_ref[rows, cols] = second.astype(BF)
        for what in range(3):
            send(i, what).start()
    for i in range(rows_here // TALL):
        for what in range(3):
            send(i, what).wait()


def body(token_grads, row_holder, row_offset, table, first_moment, second_moment):
    n_dev = lax.axis_size("dp") * lax.axis_size("vocab")
    toks, width = token_grads.shape
    rows_here = table.shape[0]
    depth = n_dev * ROWS
    lanes = 8 * CELL
    vmem = pl.BlockSpec(memory_space=pltpu.VMEM)

    with jax.named_scope("pack"):
        outgoing = pl.pallas_call(
            lambda *refs: pack_kernel(n_dev, *refs),
            out_shape=jax.ShapeDtypeStruct((depth, lanes), BF),
            in_specs=[pl.BlockSpec(memory_space=pltpu.HBM)] * 3, out_specs=vmem,
            scratch_shapes=[pltpu.VMEM((1, toks), jnp.int32), pltpu.VMEM((1, toks), jnp.int32),
                            pltpu.VMEM((toks, width), BF), pltpu.SemaphoreType.DMA((width // CELL + 2,))]
            + [pltpu.VMEM((CELL // 128 * depth, 128), F32)] * (lanes // CELL),
            compiler_params=pltpu.CompilerParams(vmem_limit_bytes=40 * 2**20),
        )(*(pltpu.with_memory_space_constraint(a, pltpu.HBM) for a in (
            row_holder.reshape(1, toks), row_offset.reshape(1, toks), token_grads)))
    with jax.named_scope("exchange"):
        arrived = lax.all_to_all(outgoing, AXES, split_axis=0, concat_axis=0, tiled=True)
    with jax.named_scope("row_sums"):
        grad_sum, part = pl.pallas_call(
            lambda *refs: sum_kernel(n_dev, *refs),
            out_shape=(jax.ShapeDtypeStruct((rows_here, width), F32),
                       jax.ShapeDtypeStruct((n_dev, 128), F32)),
            in_specs=[vmem], out_specs=(vmem, vmem),
            scratch_shapes=[pltpu.VMEM((CELL // 128 * ROWS * PITCH, 128), F32)] * (lanes // CELL),
            compiler_params=pltpu.CompilerParams(vmem_limit_bytes=40 * 2**20),
        )(arrived)
    with jax.named_scope("norm"):
        sums = lax.all_to_all(part, AXES, split_axis=0, concat_axis=0, tiled=True)
    limit = 2.0 * float(toks * n_dev * width) ** 0.5
    out = pl.BlockSpec(memory_space=pltpu.HBM)
    with jax.named_scope("adam"):
        return pl.pallas_call(
            lambda *refs: adam_kernel(limit, *refs),
            out_shape=(jax.ShapeDtypeStruct((rows_here, width), BF),) * 3,
            in_specs=[vmem] * 5, out_specs=(out,) * 3,
            scratch_shapes=[pltpu.VMEM((rows_here, width), BF)] * 3
            + [pltpu.SemaphoreType.DMA((3, rows_here // TALL))],
            compiler_params=pltpu.CompilerParams(vmem_limit_bytes=30 * 2**20),
        )(sums, grad_sum, first_moment, second_moment, table)


def solution(mesh):
    rows = P(AXES, None)
    return jax.shard_map(
        body, mesh=mesh,
        in_specs=(rows, rows, P(AXES), rows, rows, rows),
        out_specs=(rows, rows, rows), check_vma=False)
```

```python
import jax
import jax.numpy as jnp
import numpy as np
from jax import lax
from jax.experimental import pallas as pl
from jax.experimental.pallas import tpu as pltpu
from jax.sharding import PartitionSpec as P

AXES = ("dp", "vocab")
SLOTS = 3
CELL = 256
ROWS = 8
LOADS = (0, 9)
SPACING = 9
PITCH = 133
TALL = 16
WIDE = 256
BF = jnp.bfloat16
F32 = jnp.float32

OFFSETS = -1


def cell_of(piece, slot):
    if piece < 5:
        entry = 15 if piece == OFFSETS else 3 * piece + slot
        return entry // 2, 6 + entry % 2
    return (piece - 5) // 2, 3 * ((piece - 5) % 2) + slot


def iota(shape, dim):
    return lax.broadcasted_iota(jnp.int32, shape, dim)


def pack_kernel(n_dev, holder_hbm, offset_hbm, grads_hbm, out_ref, holder_ref, offset_ref, grads_ref, sems, *wide_refs):
    toks = grads_ref.shape[0]
    pieces = grads_ref.shape[1] // CELL
    moves = [pltpu.make_async_copy(a, b, sems.at[pieces + i]) for i, (a, b) in enumerate(
        ((holder_hbm, holder_ref), (offset_hbm, offset_ref)))]
    loads = {}
    ends = list(LOADS) + [pieces]
    for p, end in zip(ends, ends[1:]):
        cols = slice(p * CELL, end * CELL)
        loads[p] = pltpu.make_async_copy(grads_hbm.at[:, cols], grads_ref.at[:, cols], sems.at[p])
    for move in moves + list(loads.values())[:1]:
        move.start()
    for move in moves:
        move.wait()
    for load in list(loads.values())[1:]:
        load.start()
    columns = out_ref.shape[1] // CELL
    depth = out_ref.shape[0]
    holder = holder_ref[...]
    holder_f = holder.astype(F32)
    holder_col = jnp.broadcast_to(holder_f, (128, toks)).T
    halves = []
    for h in range(toks // 128):
        same = (holder_col == holder_f[:, h * 128:(h + 1) * 128]) & (
            iota((toks, 128), 0) < iota((toks, 128), 1) + h * 128)
        halves.append(jnp.sum(same.astype(F32), axis=0, keepdims=True))
    rank_f = jnp.concatenate(halves, axis=1)
    rank = rank_f.astype(jnp.int32)
    rank_col = jnp.broadcast_to(rank_f, (128, toks)).T
    lane = iota((toks, 128), 1).astype(F32)
    rank_hot = jnp.where(rank_col == lane, 1.0, 0.0).astype(BF)
    rank_hot = jnp.concatenate([rank_hot, jnp.zeros_like(rank_hot)], axis=1)
    offset_value = (offset_ref[...] + 1).astype(F32)
    row = iota((n_dev, toks), 0)
    hot = jnp.concatenate([
        jnp.where(row == jnp.where(rank == s, holder, -1), 1.0, 0.0).astype(BF) for s in range(SLOTS)], axis=0)
    offset_hot = jnp.where(row == holder, offset_value, 0.0).astype(BF)

    def put(piece, slot, value):
        column, r = cell_of(piece, slot)
        for c in range(0, CELL, 128):
            wide_refs[column][pl.ds(c // 128 * n_dev * SPACING + r, n_dev, stride=SPACING), :] = value[:, c:c + 128]

    done = 0
    put(OFFSETS, 0, jnp.dot(offset_hot, rank_hot, preferred_element_type=F32))
    for p in range(pieces):
        if p in loads:
            loads[p].wait()
        got = jnp.dot(hot, grads_ref[:, p * CELL:(p + 1) * CELL], preferred_element_type=F32)
        for s in range(SLOTS):
            put(p, s, got[s * n_dev:(s + 1) * n_dev])
        ready = min([cell_of(q, s)[0] for q in range(p + 1, pieces) for s in range(SLOTS)] + [columns])
        for column in range(done, ready):
            for d in range(0, n_dev, 8):
                out_ref[d * ROWS:(d + 8) * ROWS, column * CELL:(column + 1) * CELL] = jnp.concatenate([
                    jnp.concatenate([wide_refs[column][(t * n_dev + e) * SPACING:(t * n_dev + e) * SPACING + ROWS, :]
                                     for e in range(d, d + 8)], axis=0)
                    for t in range(CELL // 128)], axis=1).astype(BF)
        done = max(done, ready)


def sum_kernel(n_dev, arrived_ref, grad_ref, part_ref, *wide_refs):
    rows_here = grad_ref.shape[0]
    pieces = grad_ref.shape[1] // CELL
    columns = arrived_ref.shape[1] // CELL
    depth = arrived_ref.shape[0]

    def take(piece, slot):
        column, r = cell_of(piece, slot)
        return jnp.concatenate([
            wide_refs[column][(c // 128 * ROWS + r) * PITCH:(c // 128 * ROWS + r) * PITCH + n_dev, :]
            for c in range(0, CELL, 128)], axis=1)

    def widen(column):
        both = arrived_ref[:, column * CELL:(column + 1) * CELL].astype(F32)
        for t in range(CELL // 128):
            for source in range(n_dev):
                wide_refs[column][pl.ds(t * ROWS * PITCH + source, ROWS, stride=PITCH), :] = both[
                    source * ROWS:(source + 1) * ROWS, t * 128:(t + 1) * 128]

    widen(columns - 1)
    target = take(OFFSETS, 0)[:, :128].T.astype(jnp.int32) - 1
    row = iota((rows_here, n_dev), 0)
    hot = jnp.concatenate([
        jnp.where(row == target[s:s + 1, :], 1.0, 0.0).astype(BF) for s in range(SLOTS)], axis=1)
    total = jnp.zeros((8, CELL), F32)
    widened = 0
    for p in list(range(5, pieces)) + list(range(5)):
        need = max(cell_of(p, s)[0] for s in range(SLOTS)) + 1
        for k in range(widened, min(need, columns - 1)):
            widen(k)
        widened = max(widened, need)
        right = jnp.concatenate([take(p, s).astype(BF) for s in range(SLOTS)], axis=0)
        piece = jnp.dot(hot, right, preferred_element_type=F32)
        grad_ref[:, p * CELL:(p + 1) * CELL] = piece
        total = total + jnp.sum((piece * piece).reshape(rows_here // 8, 8, CELL), axis=0)
    folded = total[:, :128] + total[:, 128:]
    part_ref[...] = jnp.broadcast_to(jnp.sum(jnp.sum(folded, axis=0, keepdims=True), axis=1, keepdims=True), part_ref.shape)


def adam_kernel(limit, sums_ref, grad_ref, first_ref, second_ref, table_ref, ot_ref, of_ref, os_ref,
                st_ref, sf_ref, ss_ref, sems):
    rows_here, width = grad_ref.shape
    total = jnp.sum(sums_ref[...], axis=0, keepdims=True)[:, :1]
    factor = jnp.minimum(1.0, limit * lax.rsqrt(total))
    first_gain = 0.1 * factor
    second_gain = 0.05 * (factor * factor)
    root = (1.0 / (1.0 - 0.95**10)) ** 0.5
    scale = 0.02 / (1.0 - 0.9**10) / root
    tiny = 1e-8 / root

    def scaled(matrix, values):
        return jnp.dot(matrix, jnp.concatenate([values] * 3, axis=0), preferred_element_type=F32)

    def times(value):
        parts, value = [], float(np.float32(value))
        for _ in range(3):
            parts.insert(0, float(np.float32(value).astype(BF)))
            value -= parts[0]
        row, column = iota((TALL, 3 * TALL), 0), iota((TALL, 3 * TALL), 1)
        which = jnp.where(column < TALL, parts[0], jnp.where(column < 2 * TALL, parts[1], parts[2]))
        return jnp.where(row == column % TALL, which, 0.0).astype(BF)

    first_mat, second_mat = times(0.9), times(0.95)

    def send(i, what):
        rows = pl.ds(i * TALL, TALL)
        return pltpu.make_async_copy(
            (st_ref, sf_ref, ss_ref)[what].at[rows], (ot_ref, of_ref, os_ref)[what].at[rows], sems.at[what, i])

    for i in range(rows_here // TALL):
        rows = slice(i * TALL, (i + 1) * TALL)
        for c in range(0, width, WIDE):
            cols = slice(c, c + WIDE)
            grad = grad_ref[rows, cols]
            first = scaled(first_mat, first_ref[rows, cols]) + first_gain * grad
            second = scaled(second_mat, second_ref[rows, cols]) + second_gain * (grad * grad)
            bottom = second * lax.rsqrt(second) + tiny
            moved = (scale * first) * pl.reciprocal(bottom, approx=True)
            st_ref[rows, cols] = (table_ref[rows, cols].astype(F32) - moved).astype(BF)
            sf_ref[rows, cols] = first.astype(BF)
            ss_ref[rows, cols] = second.astype(BF)
        for what in range(3):
            send(i, what).start()
    for i in range(rows_here // TALL):
        for what in range(3):
            send(i, what).wait()


def body(token_grads, row_holder, row_offset, table, first_moment, second_moment):
    n_dev = lax.axis_size("dp") * lax.axis_size("vocab")
    toks, width = token_grads.shape
    rows_here = table.shape[0]
    depth = n_dev * ROWS
    lanes = 8 * CELL
    vmem = pl.BlockSpec(memory_space=pltpu.VMEM)

    with jax.named_scope("pack"):
        outgoing = pl.pallas_call(
            lambda *refs: pack_kernel(n_dev, *refs),
            out_shape=jax.ShapeDtypeStruct((depth, lanes), BF),
            in_specs=[pl.BlockSpec(memory_space=pltpu.HBM)] * 3, out_specs=vmem,
            scratch_shapes=[pltpu.VMEM((1, toks), jnp.int32), pltpu.VMEM((1, toks), jnp.int32),
                            pltpu.VMEM((toks, width), BF), pltpu.SemaphoreType.DMA((width // CELL + 2,))]
            + [pltpu.VMEM((CELL // 128 * n_dev * SPACING, 128), F32)] * (lanes // CELL),
            compiler_params=pltpu.CompilerParams(vmem_limit_bytes=40 * 2**20),
        )(*(pltpu.with_memory_space_constraint(a, pltpu.HBM) for a in (
            row_holder.reshape(1, toks), row_offset.reshape(1, toks), token_grads)))
    with jax.named_scope("exchange"):
        arrived = lax.all_to_all(outgoing, AXES, split_axis=0, concat_axis=0, tiled=True)
    with jax.named_scope("row_sums"):
        grad_sum, part = pl.pallas_call(
            lambda *refs: sum_kernel(n_dev, *refs),
            out_shape=(jax.ShapeDtypeStruct((rows_here, width), F32),
                       jax.ShapeDtypeStruct((n_dev, 128), F32)),
            in_specs=[vmem], out_specs=(vmem, vmem),
            scratch_shapes=[pltpu.VMEM((CELL // 128 * ROWS * PITCH, 128), F32)] * (lanes // CELL),
            compiler_params=pltpu.CompilerParams(vmem_limit_bytes=40 * 2**20),
        )(arrived)
    with jax.named_scope("norm"):
        sums = lax.all_to_all(part, AXES, split_axis=0, concat_axis=0, tiled=True)
    limit = 2.0 * float(toks * n_dev * width) ** 0.5
    out = pl.BlockSpec(memory_space=pltpu.HBM)
    with jax.named_scope("adam"):
        return pl.pallas_call(
            lambda *refs: adam_kernel(limit, *refs),
            out_shape=(jax.ShapeDtypeStruct((rows_here, width), BF),) * 3,
            in_specs=[vmem] * 5, out_specs=(out,) * 3,
            scratch_shapes=[pltpu.VMEM((rows_here, width), BF)] * 3
            + [pltpu.SemaphoreType.DMA((3, rows_here // TALL))],
            compiler_params=pltpu.CompilerParams(vmem_limit_bytes=30 * 2**20),
        )(sums, grad_sum, first_moment, second_moment, table)


def solution(mesh):
    rows = P(AXES, None)
    return jax.shard_map(
        body, mesh=mesh,
        in_specs=(rows, rows, P(AXES), rows, rows, rows),
        out_specs=(rows, rows, rows), check_vma=False)
```

```python
import jax
import jax.numpy as jnp
import numpy as np
from jax import lax
from jax.experimental import pallas as pl
from jax.experimental.pallas import tpu as pltpu
from jax.sharding import PartitionSpec as P

AXES = ("dp", "vocab")
SLOTS = 3
CELL = 256
ROWS = 8
LOADS = (0, 11)
SPACING = 9
PITCH = 133
TALL = 16
WIDE = 256
BF = jnp.bfloat16
F32 = jnp.float32

OFFSETS = -1


def cell_of(piece, slot):
    if piece < 5:
        entry = 15 if piece == OFFSETS else 3 * piece + slot
        return entry // 2, 6 + entry % 2
    return (piece - 5) // 2, 3 * ((piece - 5) % 2) + slot


def iota(shape, dim):
    return lax.broadcasted_iota(jnp.int32, shape, dim)


def pack_kernel(n_dev, holder_hbm, offset_hbm, grads_hbm, out_ref, holder_ref, offset_ref, grads_ref, sems, *wide_refs):
    toks = grads_ref.shape[0]
    pieces = grads_ref.shape[1] // CELL
    moves = [pltpu.make_async_copy(a, b, sems.at[pieces + i]) for i, (a, b) in enumerate(
        ((holder_hbm, holder_ref), (offset_hbm, offset_ref)))]
    loads = {}
    ends = list(LOADS) + [pieces]
    for p, end in zip(ends, ends[1:]):
        cols = slice(p * CELL, end * CELL)
        loads[p] = pltpu.make_async_copy(grads_hbm.at[:, cols], grads_ref.at[:, cols], sems.at[p])
    for move in moves + list(loads.values())[:1]:
        move.start()
    for move in moves:
        move.wait()
    for load in list(loads.values())[1:]:
        load.start()
    columns = out_ref.shape[1] // CELL
    depth = out_ref.shape[0]
    holder = holder_ref[...]
    holder_f = holder.astype(F32)
    holder_col = jnp.broadcast_to(holder_f, (128, toks)).T
    halves = []
    for h in range(toks // 128):
        same = (holder_col == holder_f[:, h * 128:(h + 1) * 128]) & (
            iota((toks, 128), 0) < iota((toks, 128), 1) + h * 128)
        halves.append(jnp.sum(same.astype(F32), axis=0, keepdims=True))
    rank_f = jnp.concatenate(halves, axis=1)
    rank = rank_f.astype(jnp.int32)
    rank_col = jnp.broadcast_to(rank_f, (128, toks)).T
    lane = iota((toks, 128), 1).astype(F32)
    rank_hot = jnp.where(rank_col == lane, 1.0, 0.0).astype(BF)
    rank_hot = jnp.concatenate([rank_hot, jnp.zeros_like(rank_hot)], axis=1)
    offset_value = (offset_ref[...] + 1).astype(F32)
    row = iota((n_dev, toks), 0)
    hot = jnp.concatenate([
        jnp.where(row == jnp.where(rank == s, holder, -1), 1.0, 0.0).astype(BF) for s in range(SLOTS)], axis=0)
    offset_hot = jnp.where(row == holder, offset_value, 0.0).astype(BF)

    def put(piece, slot, value):
        column, r = cell_of(piece, slot)
        for c in range(0, CELL, 128):
            wide_refs[column][pl.ds(c // 128 * n_dev * SPACING + r, n_dev, stride=SPACING), :] = value[:, c:c + 128]

    done = 0
    put(OFFSETS, 0, jnp.dot(offset_hot, rank_hot, preferred_element_type=F32))
    for p in range(pieces):
        if p in loads:
            loads[p].wait()
        got = jnp.dot(hot, grads_ref[:, p * CELL:(p + 1) * CELL], preferred_element_type=F32)
        for s in range(SLOTS):
            put(p, s, got[s * n_dev:(s + 1) * n_dev])
        ready = min([cell_of(q, s)[0] for q in range(p + 1, pieces) for s in range(SLOTS)] + [columns])
        for column in range(done, ready):
            for d in range(0, n_dev, 8):
                out_ref[d * ROWS:(d + 8) * ROWS, column * CELL:(column + 1) * CELL] = jnp.concatenate([
                    jnp.concatenate([wide_refs[column][(t * n_dev + e) * SPACING:(t * n_dev + e) * SPACING + ROWS, :]
                                     for e in range(d, d + 8)], axis=0)
                    for t in range(CELL // 128)], axis=1).astype(BF)
        done = max(done, ready)


def sum_kernel(n_dev, arrived_ref, grad_ref, part_ref, *wide_refs):
    rows_here = grad_ref.shape[0]
    pieces = grad_ref.shape[1] // CELL
    columns = arrived_ref.shape[1] // CELL
    depth = arrived_ref.shape[0]

    def take(piece, slot):
        column, r = cell_of(piece, slot)
        return jnp.concatenate([
            wide_refs[column][(c // 128 * ROWS + r) * PITCH:(c // 128 * ROWS + r) * PITCH + n_dev, :]
            for c in range(0, CELL, 128)], axis=1)

    def widen(column):
        both = arrived_ref[:, column * CELL:(column + 1) * CELL].astype(F32)
        for t in range(CELL // 128):
            for source in range(n_dev):
                wide_refs[column][pl.ds(t * ROWS * PITCH + source, ROWS, stride=PITCH), :] = both[
                    source * ROWS:(source + 1) * ROWS, t * 128:(t + 1) * 128]

    widen(columns - 1)
    target = take(OFFSETS, 0)[:, :128].T.astype(jnp.int32) - 1
    row = iota((rows_here, n_dev), 0)
    hot = jnp.concatenate([
        jnp.where(row == target[s:s + 1, :], 1.0, 0.0).astype(BF) for s in range(SLOTS)], axis=1)
    total = jnp.zeros((8, CELL), F32)
    widened = 0
    for p in list(range(5, pieces)) + list(range(5)):
        need = max(cell_of(p, s)[0] for s in range(SLOTS)) + 1
        for k in range(widened, min(need, columns - 1)):
            widen(k)
        widened = max(widened, need)
        right = jnp.concatenate([take(p, s).astype(BF) for s in range(SLOTS)], axis=0)
        piece = jnp.dot(hot, right, preferred_element_type=F32)
        grad_ref[:, p * CELL:(p + 1) * CELL] = piece
        total = total + jnp.sum((piece * piece).reshape(rows_here // 8, 8, CELL), axis=0)
    folded = total[:, :128] + total[:, 128:]
    part_ref[...] = jnp.broadcast_to(jnp.sum(jnp.sum(folded, axis=0, keepdims=True), axis=1, keepdims=True), part_ref.shape)


def adam_kernel(limit, sums_ref, grad_ref, first_ref, second_ref, table_ref, ot_ref, of_ref, os_ref,
                st_ref, sf_ref, ss_ref, sems):
    rows_here, width = grad_ref.shape
    total = jnp.sum(sums_ref[...], axis=0, keepdims=True)[:, :1]
    factor = jnp.minimum(1.0, limit * lax.rsqrt(total))
    first_gain = 0.1 * factor
    second_gain = 0.05 * (factor * factor)
    root = (1.0 / (1.0 - 0.95**10)) ** 0.5
    scale = 0.02 / (1.0 - 0.9**10) / root
    tiny = 1e-8 / root

    def scaled(matrix, values):
        return jnp.dot(matrix, jnp.concatenate([values] * 3, axis=0), preferred_element_type=F32)

    def times(value):
        parts, value = [], float(np.float32(value))
        for _ in range(3):
            parts.insert(0, float(np.float32(value).astype(BF)))
            value -= parts[0]
        row, column = iota((TALL, 3 * TALL), 0), iota((TALL, 3 * TALL), 1)
        which = jnp.where(column < TALL, parts[0], jnp.where(column < 2 * TALL, parts[1], parts[2]))
        return jnp.where(row == column % TALL, which, 0.0).astype(BF)

    first_mat, second_mat = times(0.9), times(0.95)

    def send(i, what):
        rows = pl.ds(i * TALL, TALL)
        return pltpu.make_async_copy(
            (st_ref, sf_ref, ss_ref)[what].at[rows], (ot_ref, of_ref, os_ref)[what].at[rows], sems.at[what, i])

    for i in range(rows_here // TALL):
        rows = slice(i * TALL, (i + 1) * TALL)
        for c in range(0, width, WIDE):
            cols = slice(c, c + WIDE)
            grad = grad_ref[rows, cols]
            first = scaled(first_mat, first_ref[rows, cols]) + first_gain * grad
            second = scaled(second_mat, second_ref[rows, cols]) + second_gain * (grad * grad)
            bottom = second * lax.rsqrt(second) + tiny
            moved = (scale * first) * pl.reciprocal(bottom, approx=True)
            st_ref[rows, cols] = (table_ref[rows, cols].astype(F32) - moved).astype(BF)
            sf_ref[rows, cols] = first.astype(BF)
            ss_ref[rows, cols] = second.astype(BF)
        for what in range(3):
            send(i, what).start()
    for i in range(rows_here // TALL):
        for what in range(3):
            send(i, what).wait()


def body(token_grads, row_holder, row_offset, table, first_moment, second_moment):
    n_dev = lax.axis_size("dp") * lax.axis_size("vocab")
    toks, width = token_grads.shape
    rows_here = table.shape[0]
    depth = n_dev * ROWS
    lanes = 8 * CELL
    vmem = pl.BlockSpec(memory_space=pltpu.VMEM)

    with jax.named_scope("pack"):
        outgoing = pl.pallas_call(
            lambda *refs: pack_kernel(n_dev, *refs),
            out_shape=jax.ShapeDtypeStruct((depth, lanes), BF),
            in_specs=[pl.BlockSpec(memory_space=pltpu.HBM)] * 3, out_specs=vmem,
            scratch_shapes=[pltpu.VMEM((1, toks), jnp.int32), pltpu.VMEM((1, toks), jnp.int32),
                            pltpu.VMEM((toks, width), BF), pltpu.SemaphoreType.DMA((width // CELL + 2,))]
            + [pltpu.VMEM((CELL // 128 * n_dev * SPACING, 128), F32)] * (lanes // CELL),
            compiler_params=pltpu.CompilerParams(vmem_limit_bytes=40 * 2**20),
        )(*(pltpu.with_memory_space_constraint(a, pltpu.HBM) for a in (
            row_holder.reshape(1, toks), row_offset.reshape(1, toks), token_grads)))
    with jax.named_scope("exchange"):
        arrived = lax.all_to_all(outgoing, AXES, split_axis=0, concat_axis=0, tiled=True)
    with jax.named_scope("row_sums"):
        grad_sum, part = pl.pallas_call(
            lambda *refs: sum_kernel(n_dev, *refs),
            out_shape=(jax.ShapeDtypeStruct((rows_here, width), F32),
                       jax.ShapeDtypeStruct((n_dev, 128), F32)),
            in_specs=[vmem], out_specs=(vmem, vmem),
            scratch_shapes=[pltpu.VMEM((CELL // 128 * ROWS * PITCH, 128), F32)] * (lanes // CELL),
            compiler_params=pltpu.CompilerParams(vmem_limit_bytes=40 * 2**20),
        )(arrived)
    with jax.named_scope("norm"):
        sums = lax.all_to_all(part, AXES, split_axis=0, concat_axis=0, tiled=True)
    limit = 2.0 * float(toks * n_dev * width) ** 0.5
    out = pl.BlockSpec(memory_space=pltpu.HBM)
    with jax.named_scope("adam"):
        return pl.pallas_call(
            lambda *refs: adam_kernel(limit, *refs),
            out_shape=(jax.ShapeDtypeStruct((rows_here, width), BF),) * 3,
            in_specs=[vmem] * 5, out_specs=(out,) * 3,
            scratch_shapes=[pltpu.VMEM((rows_here, width), BF)] * 3
            + [pltpu.SemaphoreType.DMA((3, rows_here // TALL))],
            compiler_params=pltpu.CompilerParams(vmem_limit_bytes=30 * 2**20),
        )(sums, grad_sum, first_moment, second_moment, table)


def solution(mesh):
    rows = P(AXES, None)
    return jax.shard_map(
        body, mesh=mesh,
        in_specs=(rows, rows, P(AXES), rows, rows, rows),
        out_specs=(rows, rows, rows), check_vma=False)
```
